32 devices in a mesh: groups: 2 (over x), pool: 8 (over z, y), tensor: 2 (over core).
Axes of the slice: x: 2, y: 2, z: 4, core: 2. Of those that a mesh axis runs over, the one named last changes fastest.
Arguments:
- queries: bfloat16 [16, 64, 3584], P(('groups', 'pool'), None, 'tensor'), parts along dimension 0, may hold values from -10 to 10
- new_kv: bfloat16 [16, 2, 64, 3584], P(('groups', 'pool'), None, None, 'tensor'), parts along dimension 0, may hold values from -10 to 10
- kv_pool: bfloat16 [128, 2, 32, 3584], P(('groups', 'pool'), None, None, 'tensor'), parts along dimension 0, may hold values from -10 to 10
- block_table: int32 [16, 8], P(('groups', 'pool')), parts along dimension 0, may hold values from -1 to 63, as said below
- prefix_len: int32 [16], P(('groups', 'pool')), parts along dimension 0, may hold values from 1 to 256, as said below
- out_weight: bfloat16 [3584, 7168], P('tensor', 'pool'), may hold values from -0.59765625 to 0.59765625
Outputs:
- projected: bfloat16 [1024, 7168], P(('groups', 'tensor'), 'pool'), parts along dimension 0
The draws below stay inside these ranges and needn't reach their ends.
There are 2 independent parts, one for each index of `groups`. The reference program is written for one: setup_inputs(seed, part) draws one part's arguments, and reference() takes and returns one part's arrays. A program takes and returns all parts, laid end to end along the dimension named above; an argument that names none is the same for every part. Nothing has to cross between parts.
Inputs may be any that keep to these rules, and one draw needn't show every extreme that they name: `block_table`: conversation v's first k entries are slots and the rest -1, k = ceil(prefix_len[v] / 32); no slot is named twice; the entries of one conversation lie in distinct blocks of 8 slots (distinct pool indices). `prefix_len`: some conversation has exactly 256 cached tokens.
All inputs are finite; a program needn't handle non-finite values.
Results may differ from the reference program's by a relative error of at most 0.0049.
Values may be sent and summed in bfloat16 or wider, within the bound.
A program may use at most 128 MiB of HBM per device.

```python
import jax
import jax.numpy as jnp
from jax import lax

D = 7168
ALL_HEADS = 64
HEAD_DIM = 112
HEADS = 32
BLOCK = 32
NEW = 64
CONVS = 8
MAXB = 8
SLOTS = 8
POOL_BLOCKS = 64


def conversation_plan(base_key):
    count_key, long_key, tail_key, owner_key, slot_key = jax.random.split(jax.random.fold_in(base_key, 11), 5)
    conv_ids = jnp.arange(CONVS, dtype=jnp.int32)
    counts = jax.random.randint(count_key, (CONVS,), 1, MAXB + 1)
    longest = jax.random.randint(long_key, (), 0, CONVS)
    counts = jnp.where(conv_ids == longest, MAXB, counts)
    tails = jax.random.randint(tail_key, (CONVS,), 1, BLOCK + 1)
    lengths = (counts - 1) * BLOCK + tails
    lengths = jnp.where(conv_ids == longest, MAXB * BLOCK, lengths)
    owner_order = jax.vmap(lambda single_key: jax.random.permutation(single_key, SLOTS))(jax.random.split(owner_key, CONVS))
    slot_order = jax.vmap(lambda single_key: jax.random.permutation(single_key, SLOTS))(jax.random.split(slot_key, SLOTS))
    slot_here = slot_order[owner_order, conv_ids[:, None]]
    table = owner_order * SLOTS + slot_here
    table = jnp.where(jnp.arange(MAXB, dtype=jnp.int32)[None, :] < counts[:, None], table, -1)
    return (table.astype(jnp.int32), lengths.astype(jnp.int32))


def far_rows(base_key):
    row_key, strength_key, place_key = jax.random.split(jax.random.fold_in(base_key, 7), 3)
    direction = jax.random.uniform(row_key, (CONVS, HEADS * HEAD_DIM), jnp.float32, -1.0, 1.0)
    strength = jax.random.uniform(strength_key, (CONVS, 1), jnp.float32, 5.5, 9.0)
    table, lengths = conversation_plan(base_key)
    reach = jnp.minimum(lengths, BLOCK)
    place = jax.random.randint(place_key, (CONVS,), 0, reach)
    return (direction * strength, table[:, 0], place.astype(jnp.int32))


def draw_block_table(key, part):
    table, lengths = conversation_plan(key)
    return table


def draw_prefix_len(key, part):
    table, lengths = conversation_plan(key)
    return lengths


def draw_queries(key, part):
    far_dir, far_slot, far_place = far_rows(key)
    key = jax.random.fold_in(key, 21)
    values = jnp.clip(jax.random.normal(key, (CONVS, NEW, HEADS * HEAD_DIM), jnp.float32), -6.0, 6.0)
    values = values.at[:, 0, :].set(far_dir)
    return values.astype(jnp.bfloat16)


def draw_new_kv(key, part):
    key = jax.random.fold_in(key, 37)
    values = jnp.clip(jax.random.normal(key, (CONVS, 2, NEW, HEADS * HEAD_DIM), jnp.float32), -6.0, 6.0)
    return values.astype(jnp.bfloat16)


def draw_kv_pool(key, part):
    far_dir, far_slot, far_place = far_rows(key)
    key = jax.random.fold_in(key, 43)
    values = jnp.clip(jax.random.normal(key, (POOL_BLOCKS, 2, BLOCK, HEADS * HEAD_DIM), jnp.float32), -6.0, 6.0)
    values = values.at[far_slot, 0, far_place, :].set(far_dir)
    return values.astype(jnp.bfloat16)


def levels(stream_key, dims, cuts, low, largest):
    gain = 1.0
    for position, blocks in cuts:
        heights = jax.random.uniform(jax.random.fold_in(jax.random.fold_in(stream_key, 6), position), (blocks,), jnp.float32, low / len(cuts), largest / len(cuts))
        gain = gain * jnp.repeat(jnp.exp(heights), dims[position] // blocks).reshape((-1,) + (1,) * (len(dims) - 1 - position))
    return gain


def gaussian(key, dims, width, most, cuts=(), held_as=jnp.bfloat16):
    factor_of = levels(key, dims, cuts, -0.22, 0.18) if cuts else 1.0
    array = jax.random.normal(key, dims, jnp.float32) * width * factor_of
    return jnp.minimum(jnp.maximum(array, -most), most).astype(held_as)


def setup_inputs(seed: int = 0, part: int = 0) -> dict:
    seeds = jax.random.split(jax.random.key(seed), 7)
    own_keys = jax.random.split(jax.random.fold_in(seeds[6], part), 7)
    return {
        "queries": draw_queries(jax.random.fold_in(jax.random.fold_in(seeds[6], part), 71), part),
        "new_kv": draw_new_kv(jax.random.fold_in(jax.random.fold_in(seeds[6], part), 71), part),
        "kv_pool": draw_kv_pool(jax.random.fold_in(jax.random.fold_in(seeds[6], part), 71), part),
        "block_table": draw_block_table(jax.random.fold_in(jax.random.fold_in(seeds[6], part), 71), part),
        "prefix_len": draw_prefix_len(jax.random.fold_in(jax.random.fold_in(seeds[6], part), 71), part),
        "out_weight": gaussian(seeds[5], (HEADS * HEAD_DIM, D), 0.1, 0.59765625, ((0, 2), (1, 8))),
    }


masked_fill = -1e30


def alibi_slopes(head_first, head_count):
    order = (head_first + jnp.arange(head_count, dtype=jnp.int32) + 1).astype(jnp.float32)
    return jnp.exp2(-8.0 * order / ALL_HEADS)


def block_stats(query, keys, values, query_pos, key_pos, key_limit, slopes, score_scale):
    heads = slopes.shape[0]
    query_heads = query.astype(jnp.float32).reshape(query.shape[0], heads, -1)
    key_heads = keys.astype(jnp.float32).reshape(keys.shape[0], keys.shape[1], heads, -1)
    value_heads = values.astype(jnp.float32).reshape(values.shape[0], values.shape[1], heads, -1)
    raw_scores = jnp.einsum("qhd,bkhd->bhqk", query_heads, key_heads)
    distance = (query_pos[None, None, :, None] - key_pos[:, None, None, :]).astype(jnp.float32)
    scores = raw_scores * score_scale - slopes[None, :, None, None] * distance
    usable = (key_pos[:, None, None, :] < key_limit[:, None, None, None]) & (key_pos[:, None, None, :] <= query_pos[None, None, :, None])
    masked = jnp.where(usable, scores, masked_fill)
    block_max = jnp.max(masked, axis=3)
    weights = jnp.where(usable, jnp.exp(masked - block_max[..., None]), 0.0).astype(jnp.bfloat16)
    weights = lax.optimization_barrier(weights).astype(jnp.float32)
    block_sum = jnp.sum(weights, axis=3)
    block_acc = jnp.einsum("bhqk,bkhd->bqhd", weights, value_heads)
    return block_max, block_sum, block_acc


def combine_blocks(block_max, block_sum, block_acc):
    overall = jnp.max(block_max, axis=0)
    factor = jnp.exp(block_max - overall[None])
    denom = jnp.sum(block_sum * factor, axis=0)
    numer = jnp.sum(block_acc * jnp.transpose(factor, (0, 2, 1))[..., None], axis=0)
    context = numer / jnp.transpose(denom)[..., None]
    return context.reshape(context.shape[0], -1).astype(jnp.bfloat16)


def reference(queries, new_kv, kv_pool, block_table, prefix_len, out_weight):
    slopes = alibi_slopes(ALL_HEADS - HEADS, HEADS)
    score_scale = HEAD_DIM ** -0.5

    def one_conversation(index):
        length = prefix_len[index]
        table_row = block_table[index]
        is_live = table_row >= 0
        fetched = kv_pool[jnp.where(is_live, table_row, 0)]
        own_query = queries[index]
        query_pos = length + jnp.arange(NEW, dtype=jnp.int32)
        key_pos = jnp.arange(MAXB, dtype=jnp.int32)[:, None] * BLOCK + jnp.arange(BLOCK, dtype=jnp.int32)[None, :]
        key_limit = jnp.where(is_live, length, 0).astype(jnp.int32)
        far = block_stats(own_query, fetched[:, 0], fetched[:, 1], query_pos, key_pos, key_limit, slopes, score_scale)
        near = block_stats(own_query, new_kv[index, 0][None], new_kv[index, 1][None], query_pos, query_pos[None], (length + NEW)[None], slopes, score_scale)
        joined = tuple(jnp.concatenate([first_part, second_part], axis=0) for first_part, second_part in zip(far, near))
        return combine_blocks(*joined)

    context = lax.map(one_conversation, jnp.arange(CONVS, dtype=jnp.int32))
    context = context.reshape(CONVS * NEW, HEADS * HEAD_DIM)
    return jnp.dot(context, out_weight, preferred_element_type=jnp.float32).astype(jnp.bfloat16)
```

```python
import functools

import jax
import jax.numpy as jnp
from jax import lax
from jax.experimental import pallas as pl
from jax.experimental.pallas import tpu as pltpu
from jax.sharding import PartitionSpec as P

ALL_HEADS = 64
HEAD_DIM = 112
HEADS = 32
LANES = 128
HEAD_GROUP = 8
CHUNK = HEAD_GROUP * HEAD_DIM
CHUNK_TILES = CHUNK // LANES

masked_fill = -1e30
far_away = 1 << 30
MESH = pl.DeviceIdType.MESH


def head_window(head):
    first = head * HEAD_DIM // LANES
    last = (head * HEAD_DIM + HEAD_DIM - 1) // LANES
    return first * LANES, (last - first + 1) * LANES


def kernel(
    owners, tensors, zigzag,
    table_s, length_s, table_v, q_ref, new_ref, pool_ref, w_hbm,
    out_ref,
    tbl_send, tbl_recv, tbl_smem, k_send, v_send, k_recv, v_recv,
    p_far, p_near, inv_sum, ctx, w_ref, kept, partial_send, partial_recv,
    tbl_ss, tbl_rs, k_ss, k_rs, v_ss, v_rs, ring_ss, ring_rs, part_ss, part_rs, local_sem,
):
    n = owners
    hops = n // 2
    half = n // tensors
    me = lax.axis_index("pool")
    core = lax.axis_index("tensor")
    slots = pool_ref.shape[0]
    block_len = pool_ref.shape[2]
    new_count = q_ref.shape[1]
    max_blocks = table_v.shape[1]
    chunks = q_ref.shape[2] // CHUNK
    heads_here = chunks * HEAD_GROUP
    keys = n * block_len

    w_copy = pltpu.make_async_copy(w_hbm, w_ref, local_sem.at[0])
    w_copy.start()

    barrier = pltpu.get_barrier_semaphore()
    peers = [lax.rem(me + off, n) for off in range(1, n)]
    other_core = lax.rem(core + 1, tensors)
    for d in peers:
        pl.semaphore_signal(barrier, inc=1, device_id={"pool": d}, device_id_type=MESH)
    pl.semaphore_signal(barrier, inc=1, device_id={"tensor": other_core}, device_id_type=MESH)

    tbl_send[...] = jnp.zeros_like(tbl_send)
    tbl_send[0:1, 0:max_blocks] = table_v[...]
    pl.semaphore_wait(barrier, n)

    def table_copy(d, s):
        return pltpu.make_async_remote_copy(
            src_ref=tbl_send, dst_ref=tbl_recv.at[s],
            send_sem=tbl_ss.at[d], recv_sem=tbl_rs.at[s],
            device_id={"pool": d}, device_id_type=MESH)

    for d in peers:
        table_copy(d, me).start()
    tbl_recv[me] = tbl_send[...]
    for d in peers:
        table_copy(d, d).wait_recv()
    to_smem = pltpu.make_async_copy(tbl_recv, tbl_smem, local_sem.at[1])
    to_smem.start()
    to_smem.wait()

    def wanted_slot(d):
        def step(j, slot):
            entry = tbl_smem[d, 0, j]
            hit = (entry >= 0) & (lax.div(entry, slots) == me)
            return jnp.where(hit, lax.rem(entry, slots), slot)
        slot = jnp.int32(0)
        if max_blocks <= 8:
            for j in range(max_blocks):
                slot = step(j, slot)
            return slot
        return lax.fori_loop(0, max_blocks, step, slot)

    def key_copy(d, s):
        return pltpu.make_async_remote_copy(
            src_ref=k_send.at[d], dst_ref=k_recv.at[s],
            send_sem=k_ss.at[d], recv_sem=k_rs.at[s],
            device_id={"pool": d}, device_id_type=MESH)

    def value_copy(c, d, s):
        return pltpu.make_async_remote_copy(
            src_ref=v_send.at[c, d], dst_ref=v_recv.at[c, s],
            send_sem=v_ss.at[c, d], recv_sem=v_rs.at[c, s],
            device_id={"pool": d}, device_id_type=MESH)

    wanted = [wanted_slot(d) for d in peers]
    for d, slot in zip(peers, wanted):
        k_send[d] = pool_ref[slot, 0]
        key_copy(d, me).start()
    for c in range(chunks):
        for d, slot in zip(peers, wanted):
            v_send[c, d] = pool_ref[slot, 1, :, c * CHUNK:(c + 1) * CHUNK]
            value_copy(c, d, me).start()
    own = wanted_slot(me)
    k_recv[me] = pool_ref[own, 0]
    for c in range(chunks):
        v_recv[c, me] = pool_ref[own, 1, :, c * CHUNK:(c + 1) * CHUNK]

    length = length_s[0]
    lane = lax.broadcasted_iota(jnp.int32, (new_count, keys), 1)
    row = lax.broadcasted_iota(jnp.int32, (new_count, keys), 0)
    source = lane // block_len
    offset = lane - source * block_len
    key_pos = jnp.full((new_count, keys), far_away, jnp.int32)
    for j in range(max_blocks):
        entry = table_s[0, j]
        owner = jnp.where(entry >= 0, lax.div(entry, slots), -1)
        key_pos = jnp.where(source == owner, j * block_len + offset, key_pos)
    far_ok = key_pos < length
    far_dist = (length + row - key_pos).astype(jnp.float32)
    near_row = lax.broadcasted_iota(jnp.int32, (new_count, new_count), 0)
    near_lane = lax.broadcasted_iota(jnp.int32, (new_count, new_count), 1)
    near_ok = near_lane <= near_row
    near_dist = (near_row - near_lane).astype(jnp.float32)
    score_scale = HEAD_DIM ** -0.5

    for d in peers:
        key_copy(d, d).wait_recv()

    contract_lanes = (((1,), (1,)), ((), ()))
    for c in range(chunks):
        for h in range(HEAD_GROUP):
            head = c * HEAD_GROUP + h
            first, width = head_window(h)
            window = slice(c * CHUNK + first, c * CHUNK + first + width)
            slope = jnp.float32(0)
            for t in range(tensors):
                order = ALL_HEADS - HEADS + t * heads_here + head + 1
                slope = jnp.where(core == t, jnp.float32(2.0 ** (-8.0 * order / ALL_HEADS)), slope)
            q_lane = lax.broadcasted_iota(jnp.int32, (new_count, width), 1) + first
            inside = (q_lane >= h * HEAD_DIM) & (q_lane < (h + 1) * HEAD_DIM)
            query = jnp.where(inside, q_ref[0, :, window].astype(jnp.float32), 0.0).astype(jnp.bfloat16)
            far_keys = k_recv[:, :, window].reshape(keys, width)
            far = lax.dot_general(query, far_keys, contract_lanes, preferred_element_type=jnp.float32)
            near = lax.dot_general(query, new_ref[0, 0, :, window], contract_lanes, preferred_element_type=jnp.float32)
            far = jnp.where(far_ok, far * score_scale - slope * far_dist, masked_fill)
            near = jnp.where(near_ok, near * score_scale - slope * near_dist, masked_fill)
            top = jnp.maximum(jnp.max(far, axis=1, keepdims=True), jnp.max(near, axis=1, keepdims=True))
            far = jnp.where(far_ok, jnp.exp(far - top), 0.0).astype(jnp.bfloat16)
            near = jnp.where(near_ok, jnp.exp(near - top), 0.0).astype(jnp.bfloat16)
            total = (jnp.sum(far.astype(jnp.float32), axis=1, keepdims=True)
                     + jnp.sum(near.astype(jnp.float32), axis=1, keepdims=True))
            p_far[head] = far
            p_near[head] = near
            inv_sum[head] = jnp.broadcast_to(1.0 / total, (new_count, LANES))

    def index_at(place):
        if not zigzag:
            return place
        return jnp.where(place < hops, 2 * place, 2 * (n - 1 - place) + 1)

    if zigzag:
        parity = lax.rem(me, 2)
        place = jnp.where(parity == 0, me // 2, n - 1 - me // 2)
    else:
        place = me

    def at_distance(k):
        return index_at(lax.rem(place + k + n, n))

    right, left = at_distance(1), at_distance(-1)

    def travels(way, c, k):
        return k < hops or (k == hops and c % 2 == way)

    def ring_copy(way, c, k, block):
        return pltpu.make_async_remote_copy(
            src_ref=ctx.at[block, c], dst_ref=ctx.at[block, c],
            send_sem=ring_ss.at[way, c, k - 1], recv_sem=ring_rs.at[way, c, k - 1],
            device_id={"pool": left if way else right}, device_id_type=MESH)

    for c in range(chunks):
        for d in peers:
            value_copy(c, d, d).wait_recv()
        before = None
        tiles = []
        for h in range(HEAD_GROUP):
            head = c * HEAD_GROUP + h
            first, width = head_window(h)
            far_values = v_recv[c, :, :, first:first + width].reshape(keys, width)
            near_values = new_ref[0, 1, :, c * CHUNK + first:c * CHUNK + first + width]
            acc = (jnp.dot(p_far[head], far_values, preferred_element_type=jnp.float32)
                   + jnp.dot(p_near[head], near_values, preferred_element_type=jnp.float32))
            scale = inv_sum[head]
            begin = acc[:, :LANES] * scale
            if before is not None:
                bound = h * HEAD_DIM - first
                tile_lane = lax.broadcasted_iota(jnp.int32, (new_count, LANES), 1)
                tiles.append(jnp.where(tile_lane < bound, before, begin))
            before = begin if width == LANES else acc[:, LANES:] * scale
        for i, tile in enumerate(tiles):
            ctx[me, c, :, i * LANES:(i + 1) * LANES] = tile.astype(jnp.bfloat16)
        for way in range(2):
            if travels(way, c, 1):
                ring_copy(way, c, 1, me).start()

    w_copy.wait()

    def partial_copy(i):
        return pltpu.make_async_remote_copy(
            src_ref=partial_send.at[i], dst_ref=partial_recv.at[i],
            send_sem=part_ss.at[i], recv_sem=part_rs.at[i],
            device_id={"tensor": other_core}, device_id_type=MESH)

    def hand_on(conv, value):
        part, i = conv // half, lax.rem(conv, half)

        @pl.when(part == core)
        def _():
            kept[i] = value

        @pl.when(part != core)
        def _():
            partial_send[i] = value.astype(jnp.bfloat16)
            partial_copy(i).start()

    for k in range(hops + 1):
        origins = [me] if k == 0 else [at_distance(-k), at_distance(k)]
        blocks = origins[:1] if k == hops else origins
        value = None
        for c in range(chunks):
            if k:
                for way in range(2):
                    if travels(way, c, k):
                        ring_copy(way, c, k, origins[way]).wait_recv()
                        if travels(way, c, k + 1):
                            ring_copy(way, c, k + 1, origins[way]).start()
            rows = [ctx[b, c] for b in blocks]
            rows = rows[0] if len(rows) == 1 else jnp.concatenate(rows, axis=0)
            term = jnp.dot(rows, w_ref[c * CHUNK:(c + 1) * CHUNK, :], preferred_element_type=jnp.float32)
            value = term if value is None else value + term
        for i, b in enumerate(blocks):
            hand_on(b, value[i * new_count:(i + 1) * new_count])

    for i in range(half):
        partial_copy(i).wait_recv()
        out_ref[i * new_count:(i + 1) * new_count, :] = (
            kept[i] + partial_recv[i].astype(jnp.float32)).astype(jnp.bfloat16)

    for d in peers:
        table_copy(d, me).wait_send()
        key_copy(d, me).wait_send()
        for c in range(chunks):
            value_copy(c, d, me).wait_send()
    for k in range(1, hops + 1):
        for c in range(chunks):
            for way in range(2):
                if travels(way, c, k):
                    ring_copy(way, c, k, me).wait_send()
    for i in range(half):
        partial_copy(i).wait_send()


def on_device(owners, tensors, queries, new_kv, kv_pool, block_table, prefix_len, out_weight):
    n = owners
    new_count, head_cols = queries.shape[1:]
    block_len = kv_pool.shape[2]
    columns = out_weight.shape[1]
    chunks = head_cols // CHUNK
    heads_here = chunks * HEAD_GROUP
    half = n // tensors
    hops = n // 2
    bf16, f32 = jnp.bfloat16, jnp.float32
    vmem = pl.BlockSpec(memory_space=pltpu.VMEM)
    smem = pl.BlockSpec(memory_space=pltpu.SMEM)
    dma = pltpu.SemaphoreType.DMA
    return pl.pallas_call(
        functools.partial(kernel, owners, tensors, owners <= 8),
        out_shape=jax.ShapeDtypeStruct((half * new_count, columns), bf16),
        in_specs=[smem, smem, vmem, vmem, vmem, vmem, pl.BlockSpec(memory_space=pl.ANY)],
        out_specs=vmem,
        scratch_shapes=[
            pltpu.VMEM((8, LANES), jnp.int32),
            pltpu.VMEM((n, 8, LANES), jnp.int32),
            pltpu.SMEM((n, 8, LANES), jnp.int32),
            pltpu.VMEM((n, block_len, head_cols), bf16),
            pltpu.VMEM((chunks, n, block_len, CHUNK), bf16),
            pltpu.VMEM((n, block_len, head_cols), bf16),
            pltpu.VMEM((chunks, n, block_len, CHUNK), bf16),
            pltpu.VMEM((heads_here, new_count, n * block_len), bf16),
            pltpu.VMEM((heads_here, new_count, new_count), bf16),
            pltpu.VMEM((heads_here, new_count, LANES), f32),
            pltpu.VMEM((n, chunks, new_count, CHUNK), bf16),
            pltpu.VMEM((head_cols, columns), bf16),
            pltpu.VMEM((half, new_count, columns), f32),
            pltpu.VMEM((half, new_count, columns), bf16),
            pltpu.VMEM((half, new_count, columns), bf16),
            dma((n,)), dma((n,)), dma((n,)), dma((n,)),
            dma((chunks, n)), dma((chunks, n)),
            dma((2, chunks, hops)), dma((2, chunks, hops)),
            dma((half,)), dma((half,)), dma((2,)),
        ],
        compiler_params=pltpu.CompilerParams(
            collective_id=0, has_side_effects=True, vmem_limit_bytes=60 << 20),
    )(block_table, prefix_len, block_table, queries, new_kv, kv_pool, out_weight)


def solution(mesh):
    placed = (
        P(("groups", "pool"), None, "tensor"),
        P(("groups", "pool"), None, None, "tensor"),
        P(("groups", "pool"), None, None, "tensor"),
        P(("groups", "pool"), None),
        P(("groups", "pool")),
        P("tensor", "pool"),
    )
    return jax.shard_map(
        functools.partial(on_device, mesh.shape["pool"], mesh.shape["tensor"]),
        mesh=mesh,
        in_specs=placed,
        out_specs=P(("groups", "tensor"), "pool"),
        check_vma=False,
    )
```

```python
import functools

import jax
import jax.numpy as jnp
from jax import lax
from jax.experimental import pallas as pl
from jax.experimental.pallas import tpu as pltpu
from jax.sharding import PartitionSpec as P

ALL_HEADS = 64
HEAD_DIM = 112
HEADS = 32
LANES = 128
HEAD_GROUP = 8
CHUNK = HEAD_GROUP * HEAD_DIM
CHUNK_TILES = CHUNK // LANES

masked_fill = -1e30
far_away = 1 << 30
MESH = pl.DeviceIdType.MESH


def head_window(head):
    first = head * HEAD_DIM // LANES
    last = (head * HEAD_DIM + HEAD_DIM - 1) // LANES
    return first * LANES, (last - first + 1) * LANES


def kernel(
    owners, tensors, depth,
    table_s, length_s, table_v, q_hbm, new_hbm, pool_hbm, w_hbm,
    out_ref,
    q_ref, new_ref, pool_ref, w_ref,
    tbl_send, tbl_recv, tbl_smem, k_send, v_send, k_recv, v_recv,
    p_far, p_near, inv_sum, ctx, kept, away, partial_send, partial_recv,
    tbl_ss, tbl_rs, k_ss, k_rs, v_ss, v_rs, line_ss, line_rs, side_ss, side_rs,
    part_ss, part_rs, local_sem,
):
    n = owners
    line = n // depth
    half = n // tensors
    me = lax.axis_index("pool")
    core = lax.axis_index("tensor")
    place = me // depth
    side = lax.rem(me, depth)
    slots = pool_ref.shape[0]
    block_len = pool_ref.shape[2]
    new_count = q_ref.shape[1]
    max_blocks = table_v.shape[1]
    chunks = q_ref.shape[2] // CHUNK
    heads_here = chunks * HEAD_GROUP
    keys = n * block_len

    loads = [pltpu.make_async_copy(src, dst, local_sem.at[i + 1]) for i, (src, dst) in enumerate(
        ((pool_hbm, pool_ref), (q_hbm, q_ref), (new_hbm, new_ref), (w_hbm, w_ref)))]
    for load in loads:
        load.start()

    barrier = pltpu.get_barrier_semaphore()
    peers = [lax.rem(me + off, n) for off in range(1, n)]
    other_core = lax.rem(core + 1, tensors)
    for d in peers:
        pl.semaphore_signal(barrier, inc=1, device_id={"pool": d}, device_id_type=MESH)
    pl.semaphore_signal(barrier, inc=1, device_id={"tensor": other_core}, device_id_type=MESH)

    tbl_send[...] = jnp.zeros_like(tbl_send)
    tbl_send[0:1, 0:max_blocks] = table_v[...]
    pl.semaphore_wait(barrier, n)

    def table_copy(d, s):
        return pltpu.make_async_remote_copy(
            src_ref=tbl_send, dst_ref=tbl_recv.at[s],
            send_sem=tbl_ss.at[d], recv_sem=tbl_rs.at[s],
            device_id={"pool": d}, device_id_type=MESH)

    for d in peers:
        table_copy(d, me).start()
    tbl_recv[me] = tbl_send[...]

    length = length_s[0]
    lane = lax.broadcasted_iota(jnp.int32, (new_count, keys), 1)
    row = lax.broadcasted_iota(jnp.int32, (new_count, keys), 0)
    source = lane // block_len
    offset = lane - source * block_len
    key_pos = jnp.full((new_count, keys), far_away, jnp.int32)
    for j in range(max_blocks):
        entry = table_s[0, j]
        owner = jnp.where(entry >= 0, lax.div(entry, slots), -1)
        key_pos = jnp.where(source == owner, j * block_len + offset, key_pos)
    far_ok = key_pos < length
    far_dist = (length + row - key_pos).astype(jnp.float32)
    near_row = lax.broadcasted_iota(jnp.int32, (new_count, new_count), 0)
    near_lane = lax.broadcasted_iota(jnp.int32, (new_count, new_count), 1)
    near_ok = near_lane <= near_row
    near_dist = (near_row - near_lane).astype(jnp.float32)
    score_scale = HEAD_DIM ** -0.5

    for d in peers:
        table_copy(d, d).wait_recv()
    to_smem = pltpu.make_async_copy(tbl_recv, tbl_smem, local_sem.at[0])
    to_smem.start()
    for load in loads[:3]:
        load.wait()
    to_smem.wait()

    def wanted_slot(d):
        def step(j, slot):
            entry = tbl_smem[d, 0, j]
            hit = (entry >= 0) & (lax.div(entry, slots) == me)
            return jnp.where(hit, lax.rem(entry, slots), slot)
        slot = jnp.int32(0)
        if max_blocks <= 8:
            for j in range(max_blocks):
                slot = step(j, slot)
            return slot
        return lax.fori_loop(0, max_blocks, step, slot)

    def key_copy(c, d, s):
        return pltpu.make_async_remote_copy(
            src_ref=k_send.at[c, d], dst_ref=k_recv.at[c, s],
            send_sem=k_ss.at[c, d], recv_sem=k_rs.at[c, s],
            device_id={"pool": d}, device_id_type=MESH)

    def value_copy(c, d, s):
        return pltpu.make_async_remote_copy(
            src_ref=v_send.at[c, d], dst_ref=v_recv.at[c, s],
            send_sem=v_ss.at[c, d], recv_sem=v_rs.at[c, s],
            device_id={"pool": d}, device_id_type=MESH)

    wanted = [wanted_slot(d) for d in peers]
    own = wanted_slot(me)

    def send_keys(c):
        part = slice(c * CHUNK, (c + 1) * CHUNK)
        for d, slot in zip(peers, wanted):
            k_send[c, d] = pool_ref[slot, 0, :, part]
            key_copy(c, d, me).start()
        k_recv[c, me] = pool_ref[own, 0, :, part]

    def send_values(c):
        part = slice(c * CHUNK, (c + 1) * CHUNK)
        for d, slot in zip(peers, wanted):
            v_send[c, d] = pool_ref[slot, 1, :, part]
            value_copy(c, d, me).start()
        v_recv[c, me] = pool_ref[own, 1, :, part]

    contract_lanes = (((1,), (1,)), ((), ()))

    def weigh(c):
        for d in peers:
            key_copy(c, d, d).wait_recv()
        for h in range(HEAD_GROUP):
            head = c * HEAD_GROUP + h
            first, width = head_window(h)
            window = slice(c * CHUNK + first, c * CHUNK + first + width)
            slope = jnp.float32(0)
            for t in range(tensors):
                order = ALL_HEADS - HEADS + t * heads_here + head + 1
                slope = jnp.where(core == t, jnp.float32(2.0 ** (-8.0 * order / ALL_HEADS)), slope)
            q_lane = lax.broadcasted_iota(jnp.int32, (new_count, width), 1) + first
            inside = (q_lane >= h * HEAD_DIM) & (q_lane < (h + 1) * HEAD_DIM)
            query = jnp.where(inside, q_ref[0, :, window].astype(jnp.float32), 0.0).astype(jnp.bfloat16)
            far_keys = k_recv[c, :, :, first:first + width].reshape(keys, width)
            far = lax.dot_general(query, far_keys, contract_lanes, preferred_element_type=jnp.float32)
            near = lax.dot_general(query, new_ref[0, 0, :, window], contract_lanes, preferred_element_type=jnp.float32)
            far = jnp.where(far_ok, far * score_scale - slope * far_dist, masked_fill)
            near = jnp.where(near_ok, near * score_scale - slope * near_dist, masked_fill)
            top = jnp.maximum(jnp.max(far, axis=1, keepdims=True), jnp.max(near, axis=1, keepdims=True))
            far = jnp.where(far_ok, jnp.exp(far - top), 0.0).astype(jnp.bfloat16)
            near = jnp.where(near_ok, jnp.exp(near - top), 0.0).astype(jnp.bfloat16)
            total = (jnp.sum(far.astype(jnp.float32), axis=1, keepdims=True)
                     + jnp.sum(near.astype(jnp.float32), axis=1, keepdims=True))
            p_far[head] = far
            p_near[head] = near
            inv_sum[head] = jnp.broadcast_to(1.0 / total, (new_count, LANES))

    def line_copy(c, way, origin):
        block = origin * depth + side
        goal = lax.rem(place + (line - 1 if way else 1), line) * depth + side
        return pltpu.make_async_remote_copy(
            src_ref=ctx.at[block, c], dst_ref=ctx.at[block, c],
            send_sem=line_ss.at[c, way, origin], recv_sem=line_rs.at[c, origin],
            device_id={"pool": goal}, device_id_type=MESH)

    def side_copy(c, origin, at_side):
        block = origin * depth + at_side
        return pltpu.make_async_remote_copy(
            src_ref=ctx.at[block, c], dst_ref=ctx.at[block, c],
            send_sem=side_ss.at[c, origin], recv_sem=side_rs.at[c, origin],
            device_id={"pool": place * depth + (depth - 1 - side)}, device_id_type=MESH)

    def goes_on(way):
        return place >= 1 if way else place < line - 1

    def spread(c, way, origin):
        @pl.when(goes_on(way))
        def _():
            line_copy(c, way, origin).start()

    def pass_on(c, k):
        for way in range(2):
            origin = place + k if way else place - k

            @pl.when(origin < line if way else origin >= 0)
            def _():
                line_copy(c, way, origin).wait_recv()
                spread(c, way, origin)
                if depth == 2:
                    side_copy(c, origin, side).start()

    def attend(c):
        for d in peers:
            value_copy(c, d, d).wait_recv()
        before = None
        tiles = []
        for h in range(HEAD_GROUP):
            head = c * HEAD_GROUP + h
            first, width = head_window(h)
            far_values = v_recv[c, :, :, first:first + width].reshape(keys, width)
            near_values = new_ref[0, 1, :, c * CHUNK + first:c * CHUNK + first + width]
            acc = (jnp.dot(p_far[head], far_values, preferred_element_type=jnp.float32)
                   + jnp.dot(p_near[head], near_values, preferred_element_type=jnp.float32))
            scale = inv_sum[head]
            begin = acc[:, :LANES] * scale
            if before is not None:
                bound = h * HEAD_DIM - first
                tile_lane = lax.broadcasted_iota(jnp.int32, (new_count, LANES), 1)
                tiles.append(jnp.where(tile_lane < bound, before, begin))
            before = begin if width == LANES else acc[:, LANES:] * scale
        for i, tile in enumerate(tiles):
            ctx[me, c, :, i * LANES:(i + 1) * LANES] = tile.astype(jnp.bfloat16)
        for way in range(2):
            spread(c, way, place)
        if depth == 2:
            side_copy(c, place, side).start()

    def all_there(c):
        if depth == 2:
            for origin in range(line):
                side_copy(c, origin, depth - 1 - side).wait_recv()

    pieces = 2 if half % 2 == 0 else 1
    piece = half // pieces

    def term(c, part, i):
        rows = ctx[pl.ds(part * half + i * piece, piece), c].reshape(piece * new_count, CHUNK)
        return jnp.dot(rows, w_ref[c * CHUNK:(c + 1) * CHUNK, :], preferred_element_type=jnp.float32)

    def partial_copy(i):
        return pltpu.make_async_remote_copy(
            src_ref=partial_send.at[i], dst_ref=partial_recv.at[i],
            send_sem=part_ss.at[i], recv_sem=part_rs.at[i],
            device_id={"tensor": other_core}, device_id_type=MESH)

    send_keys(0)
    send_values(0)
    for c in range(1, chunks):
        send_keys(c)
    weigh(0)
    for c in range(chunks):
        last = c == chunks - 1
        attend(c)
        if not last:
            send_values(c + 1)
            weigh(c + 1)
        if c:
            for k in range(line - 1, line):
                pass_on(c - 1, k)
            all_there(c - 1)
            if c == 1:
                loads[3].wait()
            for to, part in ((away, other_core), (kept, core)):
                for i in range(pieces):
                    to[i] = term(c - 1, part, i) if c == 1 else to[i] + term(c - 1, part, i)
        for k in range(1, line if last else line - 1):
            pass_on(c, k)
    all_there(chunks - 1)
    for i in range(pieces):
        partial_send[i] = (away[i] + term(chunks - 1, other_core, i)).astype(jnp.bfloat16)
        partial_copy(i).start()
    for i in range(pieces):
        kept[i] = kept[i] + term(chunks - 1, core, i)
    size = piece * new_count
    for i in range(pieces):
        partial_copy(i).wait_recv()
        out_ref[i * size:(i + 1) * size, :] = (
            kept[i] + partial_recv[i].astype(jnp.float32)).astype(jnp.bfloat16)

    for d in peers:
        table_copy(d, me).wait_send()
        for c in range(chunks):
            key_copy(c, d, me).wait_send()
            value_copy(c, d, me).wait_send()
    for c in range(chunks):
        for origin in range(line):
            for way in range(2):
                @pl.when(goes_on(way) & (origin >= place if way else origin <= place))
                def _():
                    line_copy(c, way, origin).wait_send()
            if depth == 2:
                side_copy(c, origin, side).wait_send()
    for i in range(pieces):
        partial_copy(i).wait_send()


def on_device(owners, tensors, queries, new_kv, kv_pool, block_table, prefix_len, out_weight):
    n = owners
    new_count, head_cols = queries.shape[1:]
    block_len = kv_pool.shape[2]
    columns = out_weight.shape[1]
    chunks = head_cols // CHUNK
    heads_here = chunks * HEAD_GROUP
    half = n // tensors
    depth = 2 if n <= 8 else 1
    line = n // depth
    pieces = 2 if half % 2 == 0 else 1
    size = half // pieces * new_count
    bf16, f32 = jnp.bfloat16, jnp.float32
    vmem = pl.BlockSpec(memory_space=pltpu.VMEM)
    smem = pl.BlockSpec(memory_space=pltpu.SMEM)
    anywhere = pl.BlockSpec(memory_space=pl.ANY)
    dma = pltpu.SemaphoreType.DMA
    blocks = pltpu.VMEM((chunks, n, block_len, CHUNK), bf16)
    return pl.pallas_call(
        functools.partial(kernel, owners, tensors, depth),
        out_shape=jax.ShapeDtypeStruct((half * new_count, columns), bf16),
        in_specs=[smem, smem, vmem, anywhere, anywhere, anywhere, anywhere],
        out_specs=vmem,
        scratch_shapes=[
            pltpu.VMEM(queries.shape, bf16),
            pltpu.VMEM(new_kv.shape, bf16),
            pltpu.VMEM(kv_pool.shape, bf16),
            pltpu.VMEM(out_weight.shape, bf16),
            pltpu.VMEM((8, LANES), jnp.int32),
            pltpu.VMEM((n, 8, LANES), jnp.int32),
            pltpu.SMEM((n, 8, LANES), jnp.int32),
            blocks, blocks, blocks, blocks,
            pltpu.VMEM((heads_here, new_count, n * block_len), bf16),
            pltpu.VMEM((heads_here, new_count, new_count), bf16),
            pltpu.VMEM((heads_here, new_count, LANES), f32),
            pltpu.VMEM((n, chunks, new_count, CHUNK), bf16),
            pltpu.VMEM((pieces, size, columns), f32),
            pltpu.VMEM((pieces, size, columns), f32),
            pltpu.VMEM((pieces, size, columns), bf16),
            pltpu.VMEM((pieces, size, columns), bf16),
            dma((n,)), dma((n,)),
            dma((chunks, n)), dma((chunks, n)), dma((chunks, n)), dma((chunks, n)),
            dma((chunks, 2, line)), dma((chunks, line)),
            dma((chunks, line)), dma((chunks, line)),
            dma((pieces,)), dma((pieces,)), dma((5,)),
        ],
        compiler_params=pltpu.CompilerParams(
            collective_id=0, has_side_effects=True, vmem_limit_bytes=60 << 20),
    )(block_table, prefix_len, block_table, queries, new_kv, kv_pool, out_weight)


def solution(mesh):
    placed = (
        P(("groups", "pool"), None, "tensor"),
        P(("groups", "pool"), None, None, "tensor"),
        P(("groups", "pool"), None, None, "tensor"),
        P(("groups", "pool"), None),
        P(("groups", "pool")),
        P("tensor", "pool"),
    )
    return jax.shard_map(
        functools.partial(on_device, mesh.shape["pool"], mesh.shape["tensor"]),
        mesh=mesh,
        in_specs=placed,
        out_specs=P(("groups", "tensor"), "pool"),
        check_vma=False,
    )
```

```python
import functools

import jax
import jax.numpy as jnp
from jax import lax
from jax.experimental import pallas as pl
from jax.experimental.pallas import tpu as pltpu
from jax.sharding import PartitionSpec as P

ALL_HEADS = 64
HEAD_DIM = 112
HEADS = 32
LANES = 128
HEAD_GROUP = 8
CHUNK = HEAD_GROUP * HEAD_DIM
CHUNK_TILES = CHUNK // LANES

masked_fill = -1e30
far_away = 1 << 30
MESH = pl.DeviceIdType.MESH


def head_window(head):
    first = head * HEAD_DIM // LANES
    last = (head * HEAD_DIM + HEAD_DIM - 1) // LANES
    return first * LANES, (last - first + 1) * LANES


def kernel(
    owners, tensors, zigzag,
    table_s, length_s, table_v, q_hbm, new_hbm, pool_hbm, w_hbm,
    out_ref,
    q_ref, new_ref, pool_ref, q_mate, stat_own, stat_send, stat_recv, acc_send, acc_recv,
    tbl_send, tbl_recv, tbl_smem, k_send, v_send, k_recv, v_recv,
    p_far, p_near, ctx, w_ref, kept, partial_send, partial_recv,
    tbl_ss, tbl_rs, k_ss, k_rs, v_ss, v_rs, ring_ss, ring_rs, part_ss, part_rs, mate_ss, mate_rs, local_sem,
):
    n = owners
    hops = n // 2
    half = n // tensors
    me = lax.axis_index("pool")
    core = lax.axis_index("tensor")
    slots = pool_ref.shape[0]
    block_len = pool_ref.shape[2]
    new_count = q_ref.shape[1]
    max_blocks = table_v.shape[1]
    chunks = q_ref.shape[2] // CHUNK
    heads_here = chunks * HEAD_GROUP
    near_n = n // 2
    keys = near_n * block_len
    base = me // near_n * near_n
    mate = lax.rem(me + near_n, n)
    convs = (me, mate)

    loads = [pltpu.make_async_copy(src, dst, local_sem.at[i + 2]) for i, (src, dst) in enumerate(
        ((q_hbm, q_ref), (pool_hbm, pool_ref), (new_hbm, new_ref)))]
    for load in loads:
        load.start()
    w_copy = pltpu.make_async_copy(w_hbm, w_ref, local_sem.at[0])
    w_copy.start()

    barrier = pltpu.get_barrier_semaphore()
    peers = [lax.rem(me + off, n) for off in range(1, n)]
    other_core = lax.rem(core + 1, tensors)
    for d in peers:
        pl.semaphore_signal(barrier, inc=1, device_id={"pool": d}, device_id_type=MESH)
    pl.semaphore_signal(barrier, inc=1, device_id={"tensor": other_core}, device_id_type=MESH)

    length = length_s[0]
    tbl_send[...] = jnp.full(tbl_send.shape, length, jnp.int32)
    tbl_send[0:1, 0:max_blocks] = table_v[...]
    pl.semaphore_wait(barrier, n)

    def table_copy(d, s):
        return pltpu.make_async_remote_copy(
            src_ref=tbl_send, dst_ref=tbl_recv.at[s],
            send_sem=tbl_ss.at[d], recv_sem=tbl_rs.at[s],
            device_id={"pool": d}, device_id_type=MESH)

    for d in peers:
        table_copy(d, me).start()
    tbl_recv[me] = tbl_send[...]

    def mate_copy(i, src, dst):
        return pltpu.make_async_remote_copy(
            src_ref=src, dst_ref=dst, send_sem=mate_ss.at[i], recv_sem=mate_rs.at[i],
            device_id={"pool": mate}, device_id_type=MESH)

    query_copy = mate_copy(0, q_ref, q_mate)
    stat_copy = mate_copy(1, stat_send, stat_recv)
    acc_copy = mate_copy(2, acc_send, acc_recv)
    loads[0].wait()
    query_copy.start()
    for d in peers:
        table_copy(d, d).wait_recv()
    to_smem = pltpu.make_async_copy(tbl_recv, tbl_smem, local_sem.at[1])
    to_smem.start()
    loads[1].wait()
    loads[2].wait()
    to_smem.wait()

    def wanted_slot(d):
        def step(j, slot):
            entry = tbl_smem[d, 0, j]
            hit = (entry >= 0) & (lax.div(entry, slots) == me)
            return jnp.where(hit, lax.rem(entry, slots), slot)
        slot = jnp.int32(0)
        if max_blocks <= 8:
            for j in range(max_blocks):
                slot = step(j, slot)
            return slot
        return lax.fori_loop(0, max_blocks, step, slot)

    def key_copy(which, d, s):
        return pltpu.make_async_remote_copy(
            src_ref=k_send.at[which, d], dst_ref=k_recv.at[which, s],
            send_sem=k_ss.at[which, d], recv_sem=k_rs.at[which, s],
            device_id={"pool": base + d}, device_id_type=MESH)

    def value_copy(which, d, s):
        return pltpu.make_async_remote_copy(
            src_ref=v_send.at[which, d], dst_ref=v_recv.at[which, s],
            send_sem=v_ss.at[which, d], recv_sem=v_rs.at[which, s],
            device_id={"pool": base + d}, device_id_type=MESH)

    here = me - base
    near_peers = [lax.rem(here + off, near_n) for off in range(1, near_n)]
    wanted = [[wanted_slot(lax.rem(base + which * near_n + d, n)) for d in near_peers] for which in range(2)]
    own = [wanted_slot(conv) for conv in convs]
    for which in (1, 0):
        for d, slot in zip(near_peers, wanted[which]):
            k_send[which, d] = pool_ref[slot, 0]
            key_copy(which, d, here).start()
    for which in (1, 0):
        for d, slot in zip(near_peers, wanted[which]):
            v_send[which, d] = pool_ref[slot, 1]
            value_copy(which, d, here).start()
    for which in range(2):
        k_recv[which, here] = pool_ref[own[which], 0]
        v_recv[which, here] = pool_ref[own[which], 1]

    lane = lax.broadcasted_iota(jnp.int32, (new_count, keys), 1)
    row = lax.broadcasted_iota(jnp.int32, (new_count, keys), 0)
    source = base + lane // block_len
    offset = lax.rem(lane, block_len)
    near_row = lax.broadcasted_iota(jnp.int32, (new_count, new_count), 0)
    near_lane = lax.broadcasted_iota(jnp.int32, (new_count, new_count), 1)
    near_ok = near_lane <= near_row
    near_dist = (near_row - near_lane).astype(jnp.float32)
    score_scale = HEAD_DIM ** -0.5
    contract_lanes = (((1,), (1,)), ((), ()))
    stat_lane = lax.broadcasted_iota(jnp.int32, (new_count, LANES), 1)

    def weigh(which):
        conv = convs[which]
        queries = (q_ref, q_mate)[which]
        conv_length = tbl_smem[conv, 1, 0]
        key_pos = jnp.full((new_count, keys), far_away, jnp.int32)
        for j in range(max_blocks):
            entry = tbl_smem[conv, 0, j]
            owner = jnp.where(entry >= 0, lax.div(entry, slots), -1)
            key_pos = jnp.where(source == owner, j * block_len + offset, key_pos)
        far_ok = key_pos < conv_length
        far_dist = (conv_length + row - key_pos).astype(jnp.float32)
        tops = jnp.zeros((new_count, LANES), jnp.float32)
        totals = jnp.ones((new_count, LANES), jnp.float32)
        for head in range(heads_here):
            c, h = divmod(head, HEAD_GROUP)
            first, width = head_window(h)
            window = slice(c * CHUNK + first, c * CHUNK + first + width)
            slope = jnp.float32(0)
            for t in range(tensors):
                order = ALL_HEADS - HEADS + t * heads_here + head + 1
                slope = jnp.where(core == t, jnp.float32(2.0 ** (-8.0 * order / ALL_HEADS)), slope)
            q_lane = lax.broadcasted_iota(jnp.int32, (new_count, width), 1) + first
            inside = (q_lane >= h * HEAD_DIM) & (q_lane < (h + 1) * HEAD_DIM)
            query = jnp.where(inside, queries[0, :, window].astype(jnp.float32), 0.0).astype(jnp.bfloat16)
            far_keys = k_recv[which, :, :, window].reshape(keys, width)
            far = lax.dot_general(query, far_keys, contract_lanes, preferred_element_type=jnp.float32)
            far = jnp.where(far_ok, far * score_scale - slope * far_dist, masked_fill)
            top = jnp.max(far, axis=1, keepdims=True)
            if which == 0:
                near = lax.dot_general(query, new_ref[0, 0, :, window], contract_lanes, preferred_element_type=jnp.float32)
                near = jnp.where(near_ok, near * score_scale - slope * near_dist, masked_fill)
                top = jnp.maximum(top, jnp.max(near, axis=1, keepdims=True))
            far = jnp.where(far_ok, jnp.exp(far - top), 0.0).astype(jnp.bfloat16)
            total = jnp.sum(far.astype(jnp.float32), axis=1, keepdims=True)
            p_far[which, head] = far
            if which == 0:
                near = jnp.where(near_ok, jnp.exp(near - top), 0.0).astype(jnp.bfloat16)
                total = total + jnp.sum(near.astype(jnp.float32), axis=1, keepdims=True)
                p_near[head] = near
            tops = jnp.where(stat_lane == head, top, tops)
            totals = jnp.where(stat_lane == head, total, totals)
        stat = (stat_own, stat_send)[which]
        stat[0] = tops
        stat[1] = totals

    def weighted(which, head):
        c, h = divmod(head, HEAD_GROUP)
        first, width = head_window(h)
        window = slice(c * CHUNK + first, c * CHUNK + first + width)
        acc = jnp.dot(p_far[which, head], v_recv[which, :, :, window].reshape(keys, width),
                      preferred_element_type=jnp.float32)
        if which == 0:
            acc = acc + jnp.dot(p_near[head], new_ref[0, 1, :, window], preferred_element_type=jnp.float32)
        return acc

    def joined(c, parts):
        tiles = []
        for h in range(1, HEAD_GROUP):
            bound = h * HEAD_DIM - head_window(h)[0]
            tiles.append(jnp.where(stat_lane < bound, parts[h - 1][:, -LANES:], parts[h][:, :LANES]))
        return tiles

    query_copy.wait_recv()
    for d in near_peers:
        key_copy(1, d, d).wait_recv()
    weigh(1)
    stat_copy.start()
    for d in near_peers:
        key_copy(0, d, d).wait_recv()
    weigh(0)
    for d in near_peers:
        value_copy(1, d, d).wait_recv()
    for c in range(chunks):
        tiles = joined(c, [weighted(1, c * HEAD_GROUP + h) for h in range(HEAD_GROUP)])
        for i, tile in enumerate(tiles):
            acc_send[:, c * CHUNK + i * LANES:c * CHUNK + (i + 1) * LANES] = tile.astype(jnp.bfloat16)
    acc_copy.start()

    def index_at(place):
        if not zigzag:
            return place
        return jnp.where(place < hops, 2 * place, 2 * (n - 1 - place) + 1)

    if zigzag:
        parity = lax.rem(me, 2)
        place = jnp.where(parity == 0, me // 2, n - 1 - me // 2)
    else:
        place = me

    def at_distance(k):
        return index_at(lax.rem(place + k + n, n))

    right, left = at_distance(1), at_distance(-1)

    def travels(way, c, k):
        return k < hops or (k == hops and c % 2 == way)

    def ring_copy(way, c, k, block):
        return pltpu.make_async_remote_copy(
            src_ref=ctx.at[block, c], dst_ref=ctx.at[block, c],
            send_sem=ring_ss.at[way, c, k - 1], recv_sem=ring_rs.at[way, c, k - 1],
            device_id={"pool": left if way else right}, device_id_type=MESH)

    for d in near_peers:
        value_copy(0, d, d).wait_recv()
    stat_copy.wait_recv()
    top = jnp.maximum(stat_own[0], stat_recv[0])
    own_part = jnp.exp(stat_own[0] - top)
    mate_part = jnp.exp(stat_recv[0] - top)
    total = own_part * stat_own[1] + mate_part * stat_recv[1]
    own_part = own_part / total
    mate_part = mate_part / total
    for c in range(chunks):
        parts, others = [], []
        for h in range(HEAD_GROUP):
            head = c * HEAD_GROUP + h
            parts.append(weighted(0, head) * own_part[:, head:head + 1])
            others.append(jnp.broadcast_to(mate_part[:, head:head + 1], (new_count, LANES)))
        if c == 0:
            acc_copy.wait_recv()
        for i, (tile, scale) in enumerate(zip(joined(c, parts), joined(c, others))):
            lanes = slice(c * CHUNK + i * LANES, c * CHUNK + (i + 1) * LANES)
            tile = tile + acc_recv[:, lanes].astype(jnp.float32) * scale
            ctx[me, c, :, i * LANES:(i + 1) * LANES] = tile.astype(jnp.bfloat16)
        for way in range(2):
            if travels(way, c, 1):
                ring_copy(way, c, 1, me).start()

    w_copy.wait()

    def partial_copy(i):
        return pltpu.make_async_remote_copy(
            src_ref=partial_send.at[i], dst_ref=partial_recv.at[i],
            send_sem=part_ss.at[i], recv_sem=part_rs.at[i],
            device_id={"tensor": other_core}, device_id_type=MESH)

    def hand_on(conv, value):
        part, i = conv // half, lax.rem(conv, half)

        @pl.when(part == core)
        def _():
            kept[i] = value

        @pl.when(part != core)
        def _():
            partial_send[i] = value.astype(jnp.bfloat16)
            partial_copy(i).start()

    for k in range(hops + 1):
        origins = [me] if k == 0 else [at_distance(-k), at_distance(k)]
        blocks = origins[:1] if k == hops else origins
        value = None
        for c in range(chunks):
            if k:
                for way in range(2):
                    if travels(way, c, k):
                        ring_copy(way, c, k, origins[way]).wait_recv()
                        if travels(way, c, k + 1):
                            ring_copy(way, c, k + 1, origins[way]).start()
            rows = [ctx[b, c] for b in blocks]
            rows = rows[0] if len(rows) == 1 else jnp.concatenate(rows, axis=0)
            term = jnp.dot(rows, w_ref[c * CHUNK:(c + 1) * CHUNK, :], preferred_element_type=jnp.float32)
            value = term if value is None else value + term
        for i, b in enumerate(blocks):
            hand_on(b, value[i * new_count:(i + 1) * new_count])

    for i in range(half):
        partial_copy(i).wait_recv()
        out_ref[i * new_count:(i + 1) * new_count, :] = (
            kept[i] + partial_recv[i].astype(jnp.float32)).astype(jnp.bfloat16)

    for d in peers:
        table_copy(d, me).wait_send()
    for which in range(2):
        for d in near_peers:
            key_copy(which, d, here).wait_send()
            value_copy(which, d, here).wait_send()
    for copy in (query_copy, stat_copy, acc_copy):
        copy.wait_send()
    for k in range(1, hops + 1):
        for c in range(chunks):
            for way in range(2):
                if travels(way, c, k):
                    ring_copy(way, c, k, me).wait_send()
    for i in range(half):
        partial_copy(i).wait_send()


def on_device(owners, tensors, queries, new_kv, kv_pool, block_table, prefix_len, out_weight):
    n = owners
    new_count, head_cols = queries.shape[1:]
    block_len = kv_pool.shape[2]
    columns = out_weight.shape[1]
    chunks = head_cols // CHUNK
    heads_here = chunks * HEAD_GROUP
    half = n // tensors
    hops = n // 2
    bf16, f32 = jnp.bfloat16, jnp.float32
    vmem = pl.BlockSpec(memory_space=pltpu.VMEM)
    smem = pl.BlockSpec(memory_space=pltpu.SMEM)
    dma = pltpu.SemaphoreType.DMA
    blocks = pltpu.VMEM((2, n // 2, block_len, head_cols), bf16)
    return pl.pallas_call(
        functools.partial(kernel, owners, tensors, owners <= 8),
        out_shape=jax.ShapeDtypeStruct((half * new_count, columns), bf16),
        in_specs=[smem, smem, vmem] + [pl.BlockSpec(memory_space=pl.ANY)] * 4,
        out_specs=vmem,
        scratch_shapes=[
            pltpu.VMEM(queries.shape, bf16),
            pltpu.VMEM(new_kv.shape, bf16),
            pltpu.VMEM(kv_pool.shape, bf16),
            pltpu.VMEM(queries.shape, bf16),
            pltpu.VMEM((2, new_count, LANES), f32),
            pltpu.VMEM((2, new_count, LANES), f32),
            pltpu.VMEM((2, new_count, LANES), f32),
            pltpu.VMEM((new_count, head_cols), bf16),
            pltpu.VMEM((new_count, head_cols), bf16),
            pltpu.VMEM((8, LANES), jnp.int32),
            pltpu.VMEM((n, 8, LANES), jnp.int32),
            pltpu.SMEM((n, 8, LANES), jnp.int32),
            blocks, blocks, blocks, blocks,
            pltpu.VMEM((2, heads_here, new_count, n // 2 * block_len), bf16),
            pltpu.VMEM((heads_here, new_count, new_count), bf16),
            pltpu.VMEM((n, chunks, new_count, CHUNK), bf16),
            pltpu.VMEM((head_cols, columns), bf16),
            pltpu.VMEM((half, new_count, columns), f32),
            pltpu.VMEM((half, new_count, columns), bf16),
            pltpu.VMEM((half, new_count, columns), bf16),
            dma((n,)), dma((n,)),
            dma((2, n // 2)), dma((2, n // 2)), dma((2, n // 2)), dma((2, n // 2)),
            dma((2, chunks, hops)), dma((2, chunks, hops)),
            dma((half,)), dma((half,)), dma((3,)), dma((3,)), dma((5,)),
        ],
        compiler_params=pltpu.CompilerParams(
            collective_id=0, has_side_effects=True, vmem_limit_bytes=60 << 20),
    )(block_table, prefix_len, block_table, queries, new_kv, kv_pool, out_weight)


def solution(mesh):
    placed = (
        P(("groups", "pool"), None, "tensor"),
        P(("groups", "pool"), None, None, "tensor"),
        P(("groups", "pool"), None, None, "tensor"),
        P(("groups", "pool"), None),
        P(("groups", "pool")),
        P("tensor", "pool"),
    )
    return jax.shard_map(
        functools.partial(on_device, mesh.shape["pool"], mesh.shape["tensor"]),
        mesh=mesh,
        in_specs=placed,
        out_specs=P(("groups", "tensor"), "pool"),
        check_vma=False,
    )
```

```python
import functools

import jax
import jax.numpy as jnp
from jax import lax
from jax.experimental import pallas as pl
from jax.experimental.pallas import tpu as pltpu
from jax.sharding import PartitionSpec as P

ALL_HEADS = 64
HEAD_DIM = 112
HEADS = 32
LANES = 128
HEAD_GROUP = 8
CHUNK = HEAD_GROUP * HEAD_DIM
CHUNK_TILES = CHUNK // LANES

masked_fill = -1e30
far_away = 1 << 30
MESH = pl.DeviceIdType.MESH


def head_window(head):
    first = head * HEAD_DIM // LANES
    last = (head * HEAD_DIM + HEAD_DIM - 1) // LANES
    return first * LANES, (last - first + 1) * LANES


def kernel(
    owners, tensors, zigzag,
    table_s, length_s, table_v, q_hbm, new_hbm, pool_hbm, w_hbm,
    out_ref,
    q_ref, new_ref, pool_ref, q_mate, stat_own, stat_send, stat_recv, acc_send, acc_recv,
    tbl_send, tbl_recv, tbl_smem, k_send, v_send, k_recv, v_recv,
    p_far, p_near, ctx, w_ref, kept, partial_send, partial_recv,
    tbl_ss, tbl_rs, k_ss, k_rs, v_ss, v_rs, ring_ss, ring_rs, part_ss, part_rs, mate_ss, mate_rs, local_sem,
):
    n = owners
    hops = n // 2
    half = n // tensors
    me = lax.axis_index("pool")
    core = lax.axis_index("tensor")
    slots = pool_ref.shape[0]
    block_len = pool_ref.shape[2]
    new_count = q_ref.shape[1]
    max_blocks = table_v.shape[1]
    chunks = q_ref.shape[2] // CHUNK
    heads_here = chunks * HEAD_GROUP
    near_n = n // 2
    keys = near_n * block_len
    base = me // near_n * near_n
    mate = lax.rem(me + near_n, n)
    convs = (me, mate)

    loads = [pltpu.make_async_copy(src, dst, local_sem.at[i + 2]) for i, (src, dst) in enumerate(
        ((q_hbm, q_ref), (pool_hbm, pool_ref), (new_hbm, new_ref)))]
    for load in loads:
        load.start()
    w_copy = pltpu.make_async_copy(w_hbm, w_ref, local_sem.at[0])
    w_copy.start()

    barrier = pltpu.get_barrier_semaphore()
    peers = [lax.rem(me + off, n) for off in range(1, n)]
    other_core = lax.rem(core + 1, tensors)
    for d in peers:
        pl.semaphore_signal(barrier, inc=1, device_id={"pool": d}, device_id_type=MESH)
    pl.semaphore_signal(barrier, inc=1, device_id={"tensor": other_core}, device_id_type=MESH)

    length = length_s[0]
    tbl_send[...] = jnp.full(tbl_send.shape, length, jnp.int32)
    tbl_send[0:1, 0:max_blocks] = table_v[...]
    pl.semaphore_wait(barrier, n)

    def table_copy(d, s):
        return pltpu.make_async_remote_copy(
            src_ref=tbl_send, dst_ref=tbl_recv.at[s],
            send_sem=tbl_ss.at[d], recv_sem=tbl_rs.at[s],
            device_id={"pool": d}, device_id_type=MESH)

    for d in peers:
        table_copy(d, me).start()
    tbl_recv[me] = tbl_send[...]

    def mate_copy(i, src, dst):
        return pltpu.make_async_remote_copy(
            src_ref=src, dst_ref=dst, send_sem=mate_ss.at[i], recv_sem=mate_rs.at[i],
            device_id={"pool": mate}, device_id_type=MESH)

    query_copy = mate_copy(0, q_ref, q_mate)
    stat_copy = mate_copy(1, stat_send, stat_recv)
    acc_copy = mate_copy(2, acc_send, acc_recv)
    loads[0].wait()
    query_copy.start()
    for d in peers:
        table_copy(d, d).wait_recv()
    to_smem = pltpu.make_async_copy(tbl_recv, tbl_smem, local_sem.at[1])
    to_smem.start()
    loads[1].wait()
    loads[2].wait()
    to_smem.wait()

    def wanted_slot(d):
        def step(j, slot):
            entry = tbl_smem[d, 0, j]
            hit = (entry >= 0) & (lax.div(entry, slots) == me)
            return jnp.where(hit, lax.rem(entry, slots), slot)
        slot = jnp.int32(0)
        if max_blocks <= 8:
            for j in range(max_blocks):
                slot = step(j, slot)
            return slot
        return lax.fori_loop(0, max_blocks, step, slot)

    def key_copy(which, d, s):
        return pltpu.make_async_remote_copy(
            src_ref=k_send.at[which, d], dst_ref=k_recv.at[which, s],
            send_sem=k_ss.at[which, d], recv_sem=k_rs.at[which, s],
            device_id={"pool": base + d}, device_id_type=MESH)

    def value_copy(which, d, s):
        return pltpu.make_async_remote_copy(
            src_ref=v_send.at[which, d], dst_ref=v_recv.at[which, s],
            send_sem=v_ss.at[which, d], recv_sem=v_rs.at[which, s],
            device_id={"pool": base + d}, device_id_type=MESH)

    here = me - base
    near_peers = [lax.rem(here + off, near_n) for off in range(1, near_n)]
    wanted = [[wanted_slot(lax.rem(base + which * near_n + d, n)) for d in near_peers] for which in range(2)]
    own = [wanted_slot(conv) for conv in convs]
    for which in (1, 0):
        for d, slot in zip(near_peers, wanted[which]):
            k_send[which, d] = pool_ref[slot, 0]
            key_copy(which, d, here).start()
        for d, slot in zip(near_peers, wanted[which]):
            v_send[which, d] = pool_ref[slot, 1]
            value_copy(which, d, here).start()
    for which in range(2):
        k_recv[which, here] = pool_ref[own[which], 0]
        v_recv[which, here] = pool_ref[own[which], 1]

    lane = lax.broadcasted_iota(jnp.int32, (new_count, keys), 1)
    row = lax.broadcasted_iota(jnp.int32, (new_count, keys), 0)
    source = base + lane // block_len
    offset = lax.rem(lane, block_len)
    near_row = lax.broadcasted_iota(jnp.int32, (new_count, new_count), 0)
    near_lane = lax.broadcasted_iota(jnp.int32, (new_count, new_count), 1)
    near_ok = near_lane <= near_row
    near_dist = (near_row - near_lane).astype(jnp.float32)
    score_scale = HEAD_DIM ** -0.5
    contract_lanes = (((1,), (1,)), ((), ()))
    stat_lane = lax.broadcasted_iota(jnp.int32, (new_count, LANES), 1)

    def weigh(which):
        conv = convs[which]
        queries = (q_ref, q_mate)[which]
        conv_length = tbl_smem[conv, 1, 0]
        key_pos = jnp.full((new_count, keys), far_away, jnp.int32)
        for j in range(max_blocks):
            entry = tbl_smem[conv, 0, j]
            owner = jnp.where(entry >= 0, lax.div(entry, slots), -1)
            key_pos = jnp.where(source == owner, j * block_len + offset, key_pos)
        far_ok = key_pos < conv_length
        far_dist = (conv_length + row - key_pos).astype(jnp.float32)
        tops = jnp.zeros((new_count, LANES), jnp.float32)
        totals = jnp.ones((new_count, LANES), jnp.float32)
        for head in range(heads_here):
            c, h = divmod(head, HEAD_GROUP)
            first, width = head_window(h)
            window = slice(c * CHUNK + first, c * CHUNK + first + width)
            slope = jnp.float32(0)
            for t in range(tensors):
                order = ALL_HEADS - HEADS + t * heads_here + head + 1
                slope = jnp.where(core == t, jnp.float32(2.0 ** (-8.0 * order / ALL_HEADS)), slope)
            q_lane = lax.broadcasted_iota(jnp.int32, (new_count, width), 1) + first
            inside = (q_lane >= h * HEAD_DIM) & (q_lane < (h + 1) * HEAD_DIM)
            query = jnp.where(inside, queries[0, :, window].astype(jnp.float32), 0.0).astype(jnp.bfloat16)
            far_keys = k_recv[which, :, :, window].reshape(keys, width)
            far = lax.dot_general(query, far_keys, contract_lanes, preferred_element_type=jnp.float32)
            far = jnp.where(far_ok, far * score_scale - slope * far_dist, masked_fill)
            top = jnp.max(far, axis=1, keepdims=True)
            if which == 0:
                near = lax.dot_general(query, new_ref[0, 0, :, window], contract_lanes, preferred_element_type=jnp.float32)
                near = jnp.where(near_ok, near * score_scale - slope * near_dist, masked_fill)
                top = jnp.maximum(top, jnp.max(near, axis=1, keepdims=True))
            far = jnp.where(far_ok, jnp.exp(far - top), 0.0).astype(jnp.bfloat16)
            total = jnp.sum(far.astype(jnp.float32), axis=1, keepdims=True)
            p_far[which, head] = far
            if which == 0:
                near = jnp.where(near_ok, jnp.exp(near - top), 0.0).astype(jnp.bfloat16)
                total = total + jnp.sum(near.astype(jnp.float32), axis=1, keepdims=True)
                p_near[head] = near
            tops = jnp.where(stat_lane == head, top, tops)
            totals = jnp.where(stat_lane == head, total, totals)
        stat = (stat_own, stat_send)[which]
        stat[0] = tops
        stat[1] = totals

    def weighted(which, head):
        c, h = divmod(head, HEAD_GROUP)
        first, width = head_window(h)
        window = slice(c * CHUNK + first, c * CHUNK + first + width)
        acc = jnp.dot(p_far[which, head], v_recv[which, :, :, window].reshape(keys, width),
                      preferred_element_type=jnp.float32)
        if which == 0:
            acc = acc + jnp.dot(p_near[head], new_ref[0, 1, :, window], preferred_element_type=jnp.float32)
        return acc

    def joined(c, parts):
        tiles = []
        for h in range(1, HEAD_GROUP):
            bound = h * HEAD_DIM - head_window(h)[0]
            tiles.append(jnp.where(stat_lane < bound, parts[h - 1][:, -LANES:], parts[h][:, :LANES]))
        return tiles

    query_copy.wait_recv()
    for d in near_peers:
        key_copy(1, d, d).wait_recv()
    weigh(1)
    stat_copy.start()
    for d in near_peers:
        value_copy(1, d, d).wait_recv()
    for c in range(chunks):
        tiles = joined(c, [weighted(1, c * HEAD_GROUP + h) for h in range(HEAD_GROUP)])
        for i, tile in enumerate(tiles):
            acc_send[:, c * CHUNK + i * LANES:c * CHUNK + (i + 1) * LANES] = tile.astype(jnp.bfloat16)
    acc_copy.start()
    for d in near_peers:
        key_copy(0, d, d).wait_recv()
    weigh(0)

    def index_at(place):
        if not zigzag:
            return place
        return jnp.where(place < hops, 2 * place, 2 * (n - 1 - place) + 1)

    if zigzag:
        parity = lax.rem(me, 2)
        place = jnp.where(parity == 0, me // 2, n - 1 - me // 2)
    else:
        place = me

    def at_distance(k):
        return index_at(lax.rem(place + k + n, n))

    right, left = at_distance(1), at_distance(-1)

    def travels(way, c, k):
        return k < hops or (k == hops and c % 2 == way)

    def ring_copy(way, c, k, block):
        return pltpu.make_async_remote_copy(
            src_ref=ctx.at[block, c], dst_ref=ctx.at[block, c],
            send_sem=ring_ss.at[way, c, k - 1], recv_sem=ring_rs.at[way, c, k - 1],
            device_id={"pool": left if way else right}, device_id_type=MESH)

    for d in near_peers:
        value_copy(0, d, d).wait_recv()
    stat_copy.wait_recv()
    top = jnp.maximum(stat_own[0], stat_recv[0])
    own_part = jnp.exp(stat_own[0] - top)
    mate_part = jnp.exp(stat_recv[0] - top)
    total = own_part * stat_own[1] + mate_part * stat_recv[1]
    own_part = own_part / total
    mate_part = mate_part / total
    for c in range(chunks):
        parts, others = [], []
        for h in range(HEAD_GROUP):
            head = c * HEAD_GROUP + h
            parts.append(weighted(0, head) * own_part[:, head:head + 1])
            others.append(jnp.broadcast_to(mate_part[:, head:head + 1], (new_count, LANES)))
        if c == 0:
            acc_copy.wait_recv()
        for i, (tile, scale) in enumerate(zip(joined(c, parts), joined(c, others))):
            lanes = slice(c * CHUNK + i * LANES, c * CHUNK + (i + 1) * LANES)
            tile = tile + acc_recv[:, lanes].astype(jnp.float32) * scale
            ctx[me, c, :, i * LANES:(i + 1) * LANES] = tile.astype(jnp.bfloat16)
        for way in range(2):
            if travels(way, c, 1):
                ring_copy(way, c, 1, me).start()

    w_copy.wait()

    def partial_copy(i):
        return pltpu.make_async_remote_copy(
            src_ref=partial_send.at[i], dst_ref=partial_recv.at[i],
            send_sem=part_ss.at[i], recv_sem=part_rs.at[i],
            device_id={"tensor": other_core}, device_id_type=MESH)

    def hand_on(conv, value):
        part, i = conv // half, lax.rem(conv, half)

        @pl.when(part == core)
        def _():
            kept[i] = value

        @pl.when(part != core)
        def _():
            partial_send[i] = value.astype(jnp.bfloat16)
            partial_copy(i).start()

    for k in range(hops + 1):
        origins = [me] if k == 0 else [at_distance(-k), at_distance(k)]
        blocks = origins[:1] if k == hops else origins
        value = None
        for c in range(chunks):
            if k:
                for way in range(2):
                    if travels(way, c, k):
                        ring_copy(way, c, k, origins[way]).wait_recv()
                        if travels(way, c, k + 1):
                            ring_copy(way, c, k + 1, origins[way]).start()
            rows = [ctx[b, c] for b in blocks]
            rows = rows[0] if len(rows) == 1 else jnp.concatenate(rows, axis=0)
            term = jnp.dot(rows, w_ref[c * CHUNK:(c + 1) * CHUNK, :], preferred_element_type=jnp.float32)
            value = term if value is None else value + term
        for i, b in enumerate(blocks):
            hand_on(b, value[i * new_count:(i + 1) * new_count])

    for i in range(half):
        partial_copy(i).wait_recv()
        out_ref[i * new_count:(i + 1) * new_count, :] = (
            kept[i] + partial_recv[i].astype(jnp.float32)).astype(jnp.bfloat16)

    for d in peers:
        table_copy(d, me).wait_send()
    for which in range(2):
        for d in near_peers:
            key_copy(which, d, here).wait_send()
            value_copy(which, d, here).wait_send()
    for copy in (query_copy, stat_copy, acc_copy):
        copy.wait_send()
    for k in range(1, hops + 1):
        for c in range(chunks):
            for way in range(2):
                if travels(way, c, k):
                    ring_copy(way, c, k, me).wait_send()
    for i in range(half):
        partial_copy(i).wait_send()


def on_device(owners, tensors, queries, new_kv, kv_pool, block_table, prefix_len, out_weight):
    n = owners
    new_count, head_cols = queries.shape[1:]
    block_len = kv_pool.shape[2]
    columns = out_weight.shape[1]
    chunks = head_cols // CHUNK
    heads_here = chunks * HEAD_GROUP
    half = n // tensors
    hops = n // 2
    bf16, f32 = jnp.bfloat16, jnp.float32
    vmem = pl.BlockSpec(memory_space=pltpu.VMEM)
    smem = pl.BlockSpec(memory_space=pltpu.SMEM)
    dma = pltpu.SemaphoreType.DMA
    blocks = pltpu.VMEM((2, n // 2, block_len, head_cols), bf16)
    return pl.pallas_call(
        functools.partial(kernel, owners, tensors, owners <= 8),
        out_shape=jax.ShapeDtypeStruct((half * new_count, columns), bf16),
        in_specs=[smem, smem, vmem] + [pl.BlockSpec(memory_space=pl.ANY)] * 4,
        out_specs=vmem,
        scratch_shapes=[
            pltpu.VMEM(queries.shape, bf16),
            pltpu.VMEM(new_kv.shape, bf16),
            pltpu.VMEM(kv_pool.shape, bf16),
            pltpu.VMEM(queries.shape, bf16),
            pltpu.VMEM((2, new_count, LANES), f32),
            pltpu.VMEM((2, new_count, LANES), f32),
            pltpu.VMEM((2, new_count, LANES), f32),
            pltpu.VMEM((new_count, head_cols), bf16),
            pltpu.VMEM((new_count, head_cols), bf16),
            pltpu.VMEM((8, LANES), jnp.int32),
            pltpu.VMEM((n, 8, LANES), jnp.int32),
            pltpu.SMEM((n, 8, LANES), jnp.int32),
            blocks, blocks, blocks, blocks,
            pltpu.VMEM((2, heads_here, new_count, n // 2 * block_len), bf16),
            pltpu.VMEM((heads_here, new_count, new_count), bf16),
            pltpu.VMEM((n, chunks, new_count, CHUNK), bf16),
            pltpu.VMEM((head_cols, columns), bf16),
            pltpu.VMEM((half, new_count, columns), f32),
            pltpu.VMEM((half, new_count, columns), bf16),
            pltpu.VMEM((half, new_count, columns), bf16),
            dma((n,)), dma((n,)),
            dma((2, n // 2)), dma((2, n // 2)), dma((2, n // 2)), dma((2, n // 2)),
            dma((2, chunks, hops)), dma((2, chunks, hops)),
            dma((half,)), dma((half,)), dma((3,)), dma((3,)), dma((5,)),
        ],
        compiler_params=pltpu.CompilerParams(
            collective_id=0, has_side_effects=True, vmem_limit_bytes=60 << 20),
    )(block_table, prefix_len, block_table, queries, new_kv, kv_pool, out_weight)


def solution(mesh):
    placed = (
        P(("groups", "pool"), None, "tensor"),
        P(("groups", "pool"), None, None, "tensor"),
        P(("groups", "pool"), None, None, "tensor"),
        P(("groups", "pool"), None),
        P(("groups", "pool")),
        P("tensor", "pool"),
    )
    return jax.shard_map(
        functools.partial(on_device, mesh.shape["pool"], mesh.shape["tensor"]),
        mesh=mesh,
        in_specs=placed,
        out_specs=P(("groups", "tensor"), "pool"),
        check_vma=False,
    )
```
